32 devices in a mesh: req: 2 (over y), ctx: 16 (over z, x, core).
Axes of the slice: x: 2, y: 2, z: 4, core: 2. Of those that a mesh axis runs over, the one named last changes fastest.
Arguments:
- query_source: bfloat16 [2304, 256], P(('req', 'ctx')), parts along dimension 0, may hold values from -32 to 32
- key_source: bfloat16 [2304, 256], P(('req', 'ctx')), parts along dimension 0, may hold values from -4 to 4
- query_edit: bfloat16 [2304, 256], P(('req', 'ctx')), parts along dimension 0, may hold values from -32 to 32
- key_edit: bfloat16 [2304, 256], P(('req', 'ctx')), parts along dimension 0, may hold values from -4 to 4
- text_count: int32 [2], P('req'), parts along dimension 0, may hold values from 72 to 288, as said below
Outputs:
- query_grad: float32 [2304, 256], P(('req', 'ctx')), parts along dimension 0
- key_grad: float32 [2304, 256], P(('req', 'ctx')), parts along dimension 0
The draws below stay inside these ranges and needn't reach their ends.
There are 2 independent parts, one for each index of `req`. The reference program is written for one: setup_inputs(seed, part) draws one part's arguments, and reference() takes and returns one part's arrays. A program takes and returns all parts, laid end to end along the dimension named above; each array names one. Nothing has to cross between parts.
Inputs may be any that keep to these rules, and one draw needn't show every extreme that they name: The first 288 positions are text slots; those at or past text_count are padding.
All inputs are finite; a program needn't handle non-finite values.
Results may differ from the reference program's by a relative error of at most 0.0095.
Values may be sent and summed in bfloat16 or wider, within the bound.
No kernel may reach another device: no remote copies, remote signals or barrier semaphores. Data moves between devices by JAX's collectives and lax.ppermute only.
A program may use at most 64 MiB of HBM per device.

```python
import math
import jax
import jax.numpy as jnp
from jax import lax

HEADS = 2
HEAD_DIM = 128
TOKENS = 1152
TEXT = 288


def draw_pair(key, offset_salt):
    base_key = jax.random.fold_in(key, offset_salt)
    first_key, second_key = jax.random.split(base_key)
    full_shape = (TOKENS, HEADS, HEAD_DIM)
    keys_all = jnp.clip(jax.random.normal(first_key, full_shape, jnp.float32), -4.0, 4.0)
    queries = jnp.clip(jax.random.normal(second_key, full_shape, jnp.float32), -4.0, 4.0)
    return (queries.reshape(TOKENS, HEADS * HEAD_DIM), keys_all.reshape(TOKENS, HEADS * HEAD_DIM))


def draw_query_source(key, part):
    return draw_pair(key, 101)[0].astype(jnp.bfloat16)


def draw_key_source(key, part):
    return draw_pair(key, 101)[1].astype(jnp.bfloat16)


def draw_query_edit(key, part):
    return draw_pair(key, 202)[0].astype(jnp.bfloat16)


def draw_key_edit(key, part):
    return draw_pair(key, 202)[1].astype(jnp.bfloat16)


def draw_text_count(key, part):
    lowest = TEXT // 4
    picked = jax.random.randint(jax.random.fold_in(key, 303), (1,), lowest, TEXT, jnp.int32)
    parity = jnp.asarray(part, jnp.int32) % 2
    return jnp.where(parity == 1, jnp.full((1,), TEXT, jnp.int32), picked).astype(jnp.int32)


def setup_inputs(seed: int = 0, part: int = 0) -> dict:
    splits = jax.random.split(jax.random.key(seed), 6)
    part_keys = jax.random.split(jax.random.fold_in(splits[5], part), 6)
    return {
        "query_source": draw_query_source(jax.random.fold_in(jax.random.fold_in(splits[5], part), 71), part),
        "key_source": draw_key_source(jax.random.fold_in(jax.random.fold_in(splits[5], part), 71), part),
        "query_edit": draw_query_edit(jax.random.fold_in(jax.random.fold_in(splits[5], part), 71), part),
        "key_edit": draw_key_edit(jax.random.fold_in(jax.random.fold_in(splits[5], part), 71), part),
        "text_count": draw_text_count(jax.random.fold_in(jax.random.fold_in(splits[5], part), 71), part),
    }


def masked_probs(scores, key_valid):
    masked = jnp.where(key_valid, scores, -jnp.inf)
    highest = lax.optimization_barrier(jnp.max(masked, axis=-1, keepdims=True))
    powers = jnp.where(key_valid, jnp.exp(scores - highest), 0.0)
    return powers / lax.optimization_barrier(jnp.sum(powers, axis=-1, keepdims=True))

def reference(query_source, key_source, query_edit, key_edit, text_count):
    score_scale = 1.0 / math.sqrt(HEAD_DIM)
    weight = 4.0 * TOKENS * math.sqrt(TOKENS)
    places = jnp.arange(TOKENS)
    token_valid = (places >= TEXT) | (places < text_count[0])
    row_weight = token_valid.astype(jnp.float32)
    block_rows = TOKENS // 8

    def split_heads(matrix):
        return matrix.reshape(TOKENS, HEADS, HEAD_DIM).transpose(1, 0, 2)

    def per_head(inputs):
        head_qs, head_ks, head_qe, head_ke = inputs
        blocks_qs = head_qs.reshape(8, block_rows, HEAD_DIM)
        blocks_qe = head_qe.reshape(8, block_rows, HEAD_DIM)
        blocks_weight = row_weight.reshape(8, block_rows, 1)

        def per_block(carry, block):
            block_qs, block_qe, block_weight = block
            scores_source = jnp.dot(block_qs, head_ks.T, preferred_element_type=jnp.float32) * score_scale
            scores_edit = jnp.dot(block_qe, head_ke.T, preferred_element_type=jnp.float32) * score_scale
            probs_source = masked_probs(scores_source, token_valid[None, :])
            probs_edit = masked_probs(scores_edit, token_valid[None, :])
            map_grad = 2.0 * weight * (probs_edit - probs_source) * block_weight
            row_delta = lax.optimization_barrier(jnp.sum(map_grad * probs_edit, axis=1, keepdims=True))
            score_grad = (probs_edit * (map_grad - row_delta)).astype(jnp.bfloat16)
            block_qgrad = jnp.dot(score_grad, head_ke, preferred_element_type=jnp.float32) * score_scale
            block_kgrad = jnp.dot(score_grad.T, block_qe, preferred_element_type=jnp.float32) * score_scale
            return (carry + block_kgrad, block_qgrad)
        start_grad = jnp.zeros((TOKENS, HEAD_DIM), jnp.float32)
        head_kgrad, head_qgrad = lax.scan(per_block, start_grad, (blocks_qs, blocks_qe, blocks_weight))
        return (head_qgrad.reshape(TOKENS, HEAD_DIM), head_kgrad)
    query_grads, key_grads = lax.map(per_head, (split_heads(query_source), split_heads(key_source), split_heads(query_edit), split_heads(key_edit)))
    query_grad = query_grads.transpose(1, 0, 2).reshape(TOKENS, HEADS * HEAD_DIM)
    key_grad = key_grads.transpose(1, 0, 2).reshape(TOKENS, HEADS * HEAD_DIM)
    return (query_grad, key_grad)
```

```python
import functools
import math

import jax
import jax.numpy as jnp
from jax import lax
from jax.experimental import pallas as pl
from jax.experimental.pallas import tpu as pltpu
from jax.sharding import PartitionSpec as P

HEAD_DIM = 128
TEXT_SLOTS = 512
GATHER_ALL_ROWS = 2048
MASKED = -1e30
VMEM = pl.BlockSpec(memory_space=pltpu.VMEM)
SMEM = pl.BlockSpec(memory_space=pltpu.SMEM)


def masked_softmax(scores, key_valid):
    masked = jnp.where(key_valid, scores, -jnp.inf)
    highest = jnp.max(masked, axis=-1, keepdims=True)
    powers = jnp.where(key_valid, jnp.exp(scores - highest), 0.0)
    totals = jnp.sum(powers, axis=-1, keepdims=True)
    return powers / totals


def local_by_rows(query_source, key_source, query_edit, key_edit, text_count):
    local_rows, full_width = query_source.shape
    head_count = full_width // HEAD_DIM
    all_rows = local_rows * lax.axis_size("ctx")
    text_slots = min(TEXT_SLOTS, all_rows // 4)
    score_scale = 1.0 / math.sqrt(HEAD_DIM)
    weight = 4.0 * all_rows * math.sqrt(all_rows)
    places = jnp.arange(all_rows)
    token_valid = (places >= text_slots) | (places < text_count[0])
    own_places = lax.axis_index("ctx") * local_rows + jnp.arange(local_rows)
    own_valid = (own_places >= text_slots) | (own_places < text_count[0])
    own_weight = own_valid.astype(jnp.float32)

    def heads_view(matrix):
        return matrix.reshape(matrix.shape[0], head_count, HEAD_DIM)

    every_ks = lax.all_gather(key_source, "ctx", axis=0, tiled=True)
    every_ke = lax.all_gather(key_edit, "ctx", axis=0, tiled=True)
    own_qs, own_qe = heads_view(query_source), heads_view(query_edit)
    dot = functools.partial(jnp.einsum, preferred_element_type=jnp.float32)
    scores_source = dot("rhd,lhd->hrl", own_qs, heads_view(every_ks)) * score_scale
    scores_edit = dot("rhd,lhd->hrl", own_qe, heads_view(every_ke)) * score_scale
    probs_source = masked_softmax(scores_source, token_valid[None, None, :])
    probs_edit = masked_softmax(scores_edit, token_valid[None, None, :])
    map_grad = 2.0 * weight * (probs_edit - probs_source) * own_weight[None, :, None]
    row_delta = jnp.sum(map_grad * probs_edit, axis=-1, keepdims=True)
    score_grad = (probs_edit * (map_grad - row_delta)).astype(jnp.bfloat16)
    query_grad = dot("hrl,lhd->rhd", score_grad, heads_view(every_ke)) * score_scale
    term_block = dot("hrl,rhd->lhd", score_grad, own_qe) * score_scale
    key_grad = lax.psum_scatter(
        term_block.reshape(all_rows, full_width), "ctx", scatter_dimension=0, tiled=True
    )
    return (query_grad.reshape(local_rows, full_width), key_grad)


def pack_kernel(head_ref, qs_ref, ks_ref, qe_ref, ke_ref, own_ref, other_ref):
    first = head_ref[0] == 0
    for place, ref in enumerate((qs_ref, ks_ref, qe_ref, ke_ref)):
        low, high = ref[:, :HEAD_DIM], ref[:, HEAD_DIM:]
        columns = slice(place * HEAD_DIM, (place + 1) * HEAD_DIM)
        own_ref[:, columns] = jnp.where(first, low, high)
        other_ref[:, columns] = jnp.where(first, high, low)


def dot_nt(a, b):
    return lax.dot_general(a, b, (((1,), (1,)), ((), ())), preferred_element_type=jnp.float32)


def fold(block, op):
    parts = [block[i : i + 8] for i in range(0, block.shape[0], 8)]
    while len(parts) > 1:
        parts = [op(*parts[i : i + 2]) if i + 1 < len(parts) else parts[i] for i in range(0, len(parts), 2)]
    return parts[0]


def head_kernel(
    weight, own_rows, a_ref, b_ref, bias_ref, live_ref, live_own_ref, query_out, key_out, scores_ref, powers_ref
):
    half = a_ref.shape[0]
    rows = 2 * half
    mine = 2 * own_rows
    scale = 1.0 / math.sqrt(HEAD_DIM)
    sharp = scale * math.log2(math.e)
    blocks = rows // mine

    def part(which, start, size):
        columns = slice(which * HEAD_DIM, (which + 1) * HEAD_DIM)
        if start + size <= half:
            return a_ref[start : start + size, columns]
        if start >= half:
            return b_ref[start - half : start - half + size, columns]
        return jnp.concatenate([a_ref[start:half, columns], b_ref[: start + size - half, columns]], axis=0)

    def queries(which, start, size):
        one = (lax.broadcasted_iota(jnp.int32, (size, HEAD_DIM), 1) == 0).astype(jnp.bfloat16)
        return jnp.concatenate([part(which, start, size), one], axis=1)

    def keys(which, start, size):
        return jnp.concatenate([part(which, start, size), bias_ref[start : start + size]], axis=1)

    def own_powers(which):
        scores = dot_nt(queries(which, 0, mine), keys(which + 1, 0, rows))
        highest = jnp.max(scores, axis=1, keepdims=True)
        powers = jnp.exp2((scores - highest) * sharp)
        return powers * (1.0 / jnp.sum(powers, axis=1, keepdims=True))

    probs_source, probs_edit = own_powers(0), own_powers(2)
    map_grad = (probs_edit - probs_source) * (2.0 * weight * live_own_ref[...])
    row_delta = jnp.sum(map_grad * probs_edit, axis=1, keepdims=True)
    grad = (probs_edit * (map_grad - row_delta)).astype(jnp.bfloat16)
    query_out[...] = jnp.dot(grad, part(3, 0, rows), preferred_element_type=jnp.float32) * scale

    chunks = []
    start = 0
    while start < rows:
        size = min(256, rows - start)
        chunks.append((start, size))
        start += size

    def score(n):
        start, size = chunks[n]
        tops = []
        for m, which in enumerate((0, 2)):
            wide = queries(which, start, size)
            top = None
            for k in range(blocks):
                block = dot_nt(keys(which + 1, k * mine, mine), wide)
                scores_ref[n % 2, m, k * mine : (k + 1) * mine, :size] = block
                high = fold(block, jnp.maximum)
                top = high if top is None else jnp.maximum(top, high)
            tops.append(jnp.max(top, axis=0, keepdims=True))
        return tops

    total = jnp.zeros((mine, HEAD_DIM), jnp.float32)
    tops = score(0)
    for n, (start, size) in enumerate(chunks):
        later = score(n + 1) if n + 1 < len(chunks) else None
        sums = [None] * 4
        for k in range(blocks):
            place = slice(k * mine, (k + 1) * mine)
            source = jnp.exp2((scores_ref[n % 2, 0, place, :size] - tops[0]) * sharp)
            edit = jnp.exp2((scores_ref[n % 2, 1, place, :size] - tops[1]) * sharp)
            if k == 0:
                powers_ref[0, :, :size] = source
                powers_ref[1, :, :size] = edit
            terms = [fold(t, jnp.add) for t in (source, edit, edit * edit, source * edit)]
            sums = [t if s is None else s + t for s, t in zip(sums, terms)]
        sum_source, sum_edit, square, cross = [jnp.sum(s, axis=0, keepdims=True) for s in sums]
        over_source, over_edit = 1.0 / sum_source, 1.0 / sum_edit
        factor = 2.0 * weight * live_ref[:, start : start + size]
        delta = factor * (square * over_edit - cross * over_source) * over_edit
        probs_edit = powers_ref[1, :, :size] * over_edit
        probs_source = powers_ref[0, :, :size] * over_source
        grad = (probs_edit * (factor * (probs_edit - probs_source) - delta)).astype(jnp.bfloat16)
        total = total + jnp.dot(grad, part(2, start, size), preferred_element_type=jnp.float32)
        tops = later
    key_out[...] = total * scale


def unpack_kernel(head_ref, query_ref, key_ref, back_ref, query_out, key_out):
    first = head_ref[0] == 0
    for place, (ref, out) in enumerate(((query_ref, query_out), (key_ref, key_out))):
        own = ref[...]
        back = back_ref[:, place * HEAD_DIM : (place + 1) * HEAD_DIM]
        out[:, :HEAD_DIM] = jnp.where(first, own, back)
        out[:, HEAD_DIM:] = jnp.where(first, back, own)


def local_by_heads(query_source, key_source, query_edit, key_edit, text_count):
    local_rows, full_width = query_source.shape
    size = lax.axis_size("ctx")
    all_rows = local_rows * size
    text_slots = min(TEXT_SLOTS, all_rows // 4)
    weight = 4.0 * all_rows * math.sqrt(all_rows)
    me = lax.axis_index("ctx")
    head = (me // 2) % 2
    head_arg = head.reshape(1).astype(jnp.int32)

    def swap(array, bits):
        return lax.ppermute(array, "ctx", [(i, i ^ bits) for i in range(size)])

    pack = jax.ShapeDtypeStruct((local_rows, 4 * HEAD_DIM), jnp.bfloat16)
    own, other = pl.pallas_call(
        pack_kernel, out_shape=(pack, pack), in_specs=[SMEM] + [VMEM] * 4, out_specs=(VMEM, VMEM), name="pack"
    )(head_arg, query_source, key_source, query_edit, key_edit)
    two = jnp.concatenate([own, swap(other, 2)], axis=0)
    held = jnp.concatenate([two] + [swap(two, bits) for bits in range(4, size, 4)], axis=0)
    across = swap(held, 1)

    order = jnp.arange(all_rows)
    half = all_rows // 2
    within = order % half
    device = me ^ (order // half) ^ (within // (2 * local_rows)) * 4 ^ (within // local_rows % 2) * 2
    place = device * local_rows + order % local_rows
    live = (place >= text_slots) | (place < text_count[0])
    bias = jnp.broadcast_to(jnp.where(live, 0.0, MASKED).astype(jnp.bfloat16)[:, None], (all_rows, HEAD_DIM))
    live_row = live.astype(jnp.float32)

    mine = 2 * local_rows
    grad = jax.ShapeDtypeStruct((mine, HEAD_DIM), jnp.float32)
    query_part, key_part = pl.pallas_call(
        functools.partial(head_kernel, weight, local_rows),
        out_shape=(grad, grad),
        in_specs=[VMEM] * 5,
        out_specs=(VMEM, VMEM),
        scratch_shapes=[
            pltpu.VMEM((2, 2, all_rows, 256), jnp.float32),
            pltpu.VMEM((2, mine, 256), jnp.float32),
        ],
        compiler_params=pltpu.CompilerParams(vmem_limit_bytes=40 * 1024 * 1024),
        name="head",
    )(held, across, bias, live_row[None, :], live_row[:mine, None])
    back = swap(jnp.concatenate([query_part[local_rows:], key_part[local_rows:]], axis=1), 2)
    out = jax.ShapeDtypeStruct((local_rows, full_width), jnp.float32)
    return pl.pallas_call(
        unpack_kernel, out_shape=(out, out), in_specs=[SMEM] + [VMEM] * 3, out_specs=(VMEM, VMEM), name="unpack"
    )(head_arg, query_part[:local_rows], key_part[:local_rows], back)


def local(query_source, key_source, query_edit, key_edit, text_count):
    local_rows, full_width = query_source.shape
    size = lax.axis_size("ctx")
    small = local_rows * size <= GATHER_ALL_ROWS
    if full_width == 2 * HEAD_DIM and small and size >= 8 and size & (size - 1) == 0 and local_rows % 8 == 0:
        return local_by_heads(query_source, key_source, query_edit, key_edit, text_count)
    return local_by_rows(query_source, key_source, query_edit, key_edit, text_count)


def solution(mesh):
    split = P(("req", "ctx"), None)
    return jax.shard_map(
        local, mesh=mesh, in_specs=(split,) * 4 + (P("req"),), out_specs=(split, split), check_vma=False
    )
```

```python
import functools
import math

import jax
import jax.numpy as jnp
from jax import lax
from jax.experimental import pallas as pl
from jax.experimental.pallas import tpu as pltpu
from jax.sharding import PartitionSpec as P

HEAD_DIM = 128
TEXT_SLOTS = 512
GATHER_ALL_ROWS = 2048
MASKED = -1e30
VMEM = pl.BlockSpec(memory_space=pltpu.VMEM)
SMEM = pl.BlockSpec(memory_space=pltpu.SMEM)
HBM = pl.BlockSpec(memory_space=pltpu.HBM)


def masked_softmax(scores, key_valid):
    masked = jnp.where(key_valid, scores, -jnp.inf)
    highest = jnp.max(masked, axis=-1, keepdims=True)
    powers = jnp.where(key_valid, jnp.exp(scores - highest), 0.0)
    totals = jnp.sum(powers, axis=-1, keepdims=True)
    return powers / totals


def local_by_rows(query_source, key_source, query_edit, key_edit, text_count):
    local_rows, full_width = query_source.shape
    head_count = full_width // HEAD_DIM
    all_rows = local_rows * lax.axis_size("ctx")
    text_slots = min(TEXT_SLOTS, all_rows // 4)
    score_scale = 1.0 / math.sqrt(HEAD_DIM)
    weight = 4.0 * all_rows * math.sqrt(all_rows)
    places = jnp.arange(all_rows)
    token_valid = (places >= text_slots) | (places < text_count[0])
    own_places = lax.axis_index("ctx") * local_rows + jnp.arange(local_rows)
    own_valid = (own_places >= text_slots) | (own_places < text_count[0])
    own_weight = own_valid.astype(jnp.float32)

    def heads_view(matrix):
        return matrix.reshape(matrix.shape[0], head_count, HEAD_DIM)

    every_ks = lax.all_gather(key_source, "ctx", axis=0, tiled=True)
    every_ke = lax.all_gather(key_edit, "ctx", axis=0, tiled=True)
    own_qs, own_qe = heads_view(query_source), heads_view(query_edit)
    dot = functools.partial(jnp.einsum, preferred_element_type=jnp.float32)
    scores_source = dot("rhd,lhd->hrl", own_qs, heads_view(every_ks)) * score_scale
    scores_edit = dot("rhd,lhd->hrl", own_qe, heads_view(every_ke)) * score_scale
    probs_source = masked_softmax(scores_source, token_valid[None, None, :])
    probs_edit = masked_softmax(scores_edit, token_valid[None, None, :])
    map_grad = 2.0 * weight * (probs_edit - probs_source) * own_weight[None, :, None]
    row_delta = jnp.sum(map_grad * probs_edit, axis=-1, keepdims=True)
    score_grad = (probs_edit * (map_grad - row_delta)).astype(jnp.bfloat16)
    query_grad = dot("hrl,lhd->rhd", score_grad, heads_view(every_ke)) * score_scale
    term_block = dot("hrl,rhd->lhd", score_grad, own_qe) * score_scale
    key_grad = lax.psum_scatter(
        term_block.reshape(all_rows, full_width), "ctx", scatter_dimension=0, tiled=True
    )
    return (query_grad.reshape(local_rows, full_width), key_grad)


def pack_kernel(head_ref, qs_ref, ks_ref, qe_ref, ke_ref, own_ref, other_ref, held_ref, sems):
    copies = [
        pltpu.make_async_copy(ref, held_ref.at[place], sems.at[place])
        for place, ref in enumerate((qs_ref, ks_ref, qe_ref, ke_ref))
    ]
    for copy in copies:
        copy.start()
    first = head_ref[0] == 0
    for place, copy in enumerate(copies):
        copy.wait()
        low, high = held_ref[place, :, :HEAD_DIM], held_ref[place, :, HEAD_DIM:]
        columns = slice(place * HEAD_DIM, (place + 1) * HEAD_DIM)
        own_ref[:, columns] = jnp.where(first, low, high)
        other_ref[:, columns] = jnp.where(first, high, low)


def dot_nt(a, b):
    return lax.dot_general(a, b, (((1,), (1,)), ((), ())), preferred_element_type=jnp.float32)


def fold(block, op):
    parts = [block[i : i + 8] for i in range(0, block.shape[0], 8)]
    while len(parts) > 1:
        parts = [op(*parts[i : i + 2]) if i + 1 < len(parts) else parts[i] for i in range(0, len(parts), 2)]
    return parts[0]


def head_kernel(
    weight, own_rows, a_ref, b_ref, bias_ref, live_ref, live_own_ref, keep_out, send_out, scores_ref, powers_ref
):
    half = a_ref.shape[0]
    rows = 2 * half
    mine = 2 * own_rows
    scale = 1.0 / math.sqrt(HEAD_DIM)
    sharp = scale * math.log2(math.e)
    blocks = rows // mine

    def part(which, start, size):
        columns = slice(which * HEAD_DIM, (which + 1) * HEAD_DIM)
        if start + size <= half:
            return a_ref[start : start + size, columns]
        if start >= half:
            return b_ref[start - half : start - half + size, columns]
        return jnp.concatenate([a_ref[start:half, columns], b_ref[: start + size - half, columns]], axis=0)

    def queries(which, start, size):
        one = (lax.broadcasted_iota(jnp.int32, (size, HEAD_DIM), 1) == 0).astype(jnp.bfloat16)
        return jnp.concatenate([part(which, start, size), one], axis=1)

    def keys(which, start, size):
        return jnp.concatenate([part(which, start, size), bias_ref[start : start + size]], axis=1)

    def own_powers(which):
        scores = dot_nt(queries(which, 0, mine), keys(which + 1, 0, rows))
        highest = jnp.max(scores, axis=1, keepdims=True)
        powers = jnp.exp2((scores - highest) * sharp)
        return powers * (1.0 / jnp.sum(powers, axis=1, keepdims=True))

    probs_source, probs_edit = own_powers(0), own_powers(2)
    map_grad = (probs_edit - probs_source) * (2.0 * weight * live_own_ref[...])
    row_delta = jnp.sum(map_grad * probs_edit, axis=1, keepdims=True)
    grad = (probs_edit * (map_grad - row_delta)).astype(jnp.bfloat16)
    query_grad = jnp.dot(grad, part(3, 0, rows), preferred_element_type=jnp.float32) * scale

    chunks = []
    start = 0
    while start < rows:
        size = min(256, rows - start)
        chunks.append((start, size))
        start += size

    def score(n):
        start, size = chunks[n]
        tops = []
        for m, which in enumerate((0, 2)):
            wide = queries(which, start, size)
            top = None
            for k in range(0, rows, half):
                block = dot_nt(keys(which + 1, k, half), wide)
                scores_ref[n % 2, m, k : k + half, :size] = block
                high = fold(block, jnp.maximum)
                top = high if top is None else jnp.maximum(top, high)
            tops.append(jnp.max(top, axis=0, keepdims=True))
        return tops

    total = jnp.zeros((mine, HEAD_DIM), jnp.float32)
    tops = score(0)
    for n, (start, size) in enumerate(chunks):
        later = score(n + 1) if n + 1 < len(chunks) else None
        sums = [None] * 4
        for k in range(blocks):
            place = slice(k * mine, (k + 1) * mine)
            source = jnp.exp2((scores_ref[n % 2, 0, place, :size] - tops[0]) * sharp)
            edit = jnp.exp2((scores_ref[n % 2, 1, place, :size] - tops[1]) * sharp)
            if k == 0:
                powers_ref[0, :, :size] = source
                powers_ref[1, :, :size] = edit
            terms = [fold(t, jnp.add) for t in (source, edit, edit * edit, source * edit)]
            sums = [t if s is None else s + t for s, t in zip(sums, terms)]
        sum_source, sum_edit, square, cross = [jnp.sum(s, axis=0, keepdims=True) for s in sums]
        over_source, over_edit = 1.0 / sum_source, 1.0 / sum_edit
        factor = 2.0 * weight * live_ref[:, start : start + size]
        delta = factor * (square * over_edit - cross * over_source) * over_edit
        probs_edit = powers_ref[1, :, :size] * over_edit
        probs_source = powers_ref[0, :, :size] * over_source
        grad = (probs_edit * (factor * (probs_edit - probs_source) - delta)).astype(jnp.bfloat16)
        total = total + jnp.dot(grad, part(2, start, size), preferred_element_type=jnp.float32)
        tops = later
    for columns, grad in ((slice(None, HEAD_DIM), query_grad), (slice(HEAD_DIM, None), total * scale)):
        keep_out[:, columns] = grad[:own_rows]
        send_out[:, columns] = grad[own_rows:]


def local_by_heads(query_source, key_source, query_edit, key_edit, text_count):
    local_rows, full_width = query_source.shape
    size = lax.axis_size("ctx")
    all_rows = local_rows * size
    text_slots = min(TEXT_SLOTS, all_rows // 4)
    weight = 4.0 * all_rows * math.sqrt(all_rows)
    me = lax.axis_index("ctx")
    head = (me >> 1) & 1
    arrays = (query_source, key_source, query_edit, key_edit)

    def swap(array, bits):
        return lax.ppermute(array, "ctx", [(i, i ^ bits) for i in range(size)])

    pack = jax.ShapeDtypeStruct((local_rows, 4 * HEAD_DIM), jnp.bfloat16)
    own, other = pl.pallas_call(
        pack_kernel,
        out_shape=(pack, pack),
        in_specs=[SMEM] + [HBM] * 4,
        out_specs=(VMEM, VMEM),
        scratch_shapes=[pltpu.VMEM((4, local_rows, full_width), jnp.bfloat16), pltpu.SemaphoreType.DMA((4,))],
        compiler_params=pltpu.CompilerParams(vmem_limit_bytes=4 * 1024 * 1024),
        name="pack",
    )(head.reshape(1), *(pltpu.with_memory_space_constraint(x, pltpu.HBM) for x in arrays))

    mine = 2 * local_rows
    order = jnp.arange(all_rows)
    half = all_rows // 2
    within = order % half
    device = me ^ (order // half) ^ (within // mine) * 4 ^ (within // local_rows % 2) * 2
    place = device * local_rows + order % local_rows
    live = (place >= text_slots) | (place < text_count[0])
    bias = jnp.broadcast_to(jnp.where(live, 0.0, MASKED).astype(jnp.bfloat16)[:, None], (all_rows, HEAD_DIM))
    live_row = live.astype(jnp.float32)
    live_own = live_row[:mine, None]

    partner, bias, live_row, live_own = lax.optimization_barrier(
        (swap(other, 2), bias, live_row[None, :], live_own)
    )
    two = jnp.concatenate([own, partner], axis=0)
    far = [(0, own), (local_rows, partner)]
    for bit in [1 << p for p in range(size.bit_length() - 2, 2, -1)]:
        far += [(at + bit * mine // 4, swap(block, bit)) for at, block in far]
    far = far[2:]
    blocks = [(0, two), (mine, swap(two, 4))] + far + [(at + mine, swap(block, 4)) for at, block in far]
    held = jnp.concatenate([block for _, block in sorted(blocks, key=lambda entry: entry[0])], axis=0)

    grads = jax.ShapeDtypeStruct((local_rows, 2 * HEAD_DIM), jnp.float32)
    keep, send = pl.pallas_call(
        functools.partial(head_kernel, weight, local_rows),
        out_shape=(grads, grads),
        in_specs=[VMEM] * 5,
        out_specs=(VMEM, VMEM),
        scratch_shapes=[
            pltpu.VMEM((2, 2, all_rows, 256), jnp.float32),
            pltpu.VMEM((2, mine, 256), jnp.float32),
        ],
        compiler_params=pltpu.CompilerParams(vmem_limit_bytes=40 * 1024 * 1024),
        name="head",
    )(held, swap(held, 1), bias, live_row, live_own)
    back = swap(send, 2)

    def both_heads(columns):
        mine, other = keep[:, columns], back[:, columns]
        return jnp.where(
            head == 0, jnp.concatenate([mine, other], axis=1), jnp.concatenate([other, mine], axis=1)
        )

    return both_heads(slice(None, HEAD_DIM)), both_heads(slice(HEAD_DIM, None))


def local(query_source, key_source, query_edit, key_edit, text_count):
    local_rows, full_width = query_source.shape
    size = lax.axis_size("ctx")
    small = local_rows * size <= GATHER_ALL_ROWS
    if full_width == 2 * HEAD_DIM and small and size >= 8 and size & (size - 1) == 0 and local_rows % 8 == 0:
        return local_by_heads(query_source, key_source, query_edit, key_edit, text_count)
    return local_by_rows(query_source, key_source, query_edit, key_edit, text_count)


def solution(mesh):
    split = P(("req", "ctx"), None)
    return jax.shard_map(
        local, mesh=mesh, in_specs=(split,) * 4 + (P("req"),), out_specs=(split, split), check_vma=False
    )
```

```python
import functools
import math

import jax
import jax.numpy as jnp
from jax import lax
from jax.experimental import pallas as pl
from jax.experimental.pallas import tpu as pltpu
from jax.sharding import PartitionSpec as P

HEAD_DIM = 128
TEXT_SLOTS = 512
GATHER_ALL_ROWS = 2048
MASKED = -1e30
ROW_CHUNK = 256
SHARP = math.log2(math.e) / math.sqrt(HEAD_DIM)
VMEM = pl.BlockSpec(memory_space=pltpu.VMEM)
SMEM = pl.BlockSpec(memory_space=pltpu.SMEM)
HBM = pl.BlockSpec(memory_space=pltpu.HBM)


def masked_softmax(scores, key_valid):
    masked = jnp.where(key_valid, scores, -jnp.inf)
    highest = jnp.max(masked, axis=-1, keepdims=True)
    powers = jnp.where(key_valid, jnp.exp(scores - highest), 0.0)
    totals = jnp.sum(powers, axis=-1, keepdims=True)
    return powers / totals


def local_by_rows(query_source, key_source, query_edit, key_edit, text_count):
    local_rows, full_width = query_source.shape
    head_count = full_width // HEAD_DIM
    all_rows = local_rows * lax.axis_size("ctx")
    text_slots = min(TEXT_SLOTS, all_rows // 4)
    score_scale = 1.0 / math.sqrt(HEAD_DIM)
    weight = 4.0 * all_rows * math.sqrt(all_rows)
    places = jnp.arange(all_rows)
    token_valid = (places >= text_slots) | (places < text_count[0])
    own_places = lax.axis_index("ctx") * local_rows + jnp.arange(local_rows)
    own_valid = (own_places >= text_slots) | (own_places < text_count[0])
    own_weight = own_valid.astype(jnp.float32)

    def heads_view(matrix):
        return matrix.reshape(matrix.shape[0], head_count, HEAD_DIM)

    every_ks = lax.all_gather(key_source, "ctx", axis=0, tiled=True)
    every_ke = lax.all_gather(key_edit, "ctx", axis=0, tiled=True)
    own_qs, own_qe = heads_view(query_source), heads_view(query_edit)
    dot = functools.partial(jnp.einsum, preferred_element_type=jnp.float32)
    scores_source = dot("rhd,lhd->hrl", own_qs, heads_view(every_ks)) * score_scale
    scores_edit = dot("rhd,lhd->hrl", own_qe, heads_view(every_ke)) * score_scale
    probs_source = masked_softmax(scores_source, token_valid[None, None, :])
    probs_edit = masked_softmax(scores_edit, token_valid[None, None, :])
    map_grad = 2.0 * weight * (probs_edit - probs_source) * own_weight[None, :, None]
    row_delta = jnp.sum(map_grad * probs_edit, axis=-1, keepdims=True)
    score_grad = (probs_edit * (map_grad - row_delta)).astype(jnp.bfloat16)
    query_grad = dot("hrl,lhd->rhd", score_grad, heads_view(every_ke)) * score_scale
    term_block = dot("hrl,rhd->lhd", score_grad, own_qe) * score_scale
    key_grad = lax.psum_scatter(
        term_block.reshape(all_rows, full_width), "ctx", scatter_dimension=0, tiled=True
    )
    return (query_grad.reshape(local_rows, full_width), key_grad)


def pack_kernel(qs_ref, ks_ref, qe_ref, ke_ref, own_ref, other_ref, held_ref, sems):
    copies = [
        pltpu.make_async_copy(ref, held_ref.at[place], sems.at[place])
        for place, ref in enumerate((qs_ref, ks_ref, qe_ref, ke_ref))
    ]
    for copy in copies:
        copy.start()
    first = (lax.axis_index("ctx") >> 1) & 1 == 0
    for place, copy in enumerate(copies):
        copy.wait()
        low, high = held_ref[place, :, :HEAD_DIM], held_ref[place, :, HEAD_DIM:]
        columns = slice(place * HEAD_DIM, (place + 1) * HEAD_DIM)
        own_ref[:, columns] = jnp.where(first, low, high)
        other_ref[:, columns] = jnp.where(first, high, low)


def mask_kernel(own_rows, text_slots, count_ref, bias_ref, live_ref, live_own_ref):
    me = lax.axis_index("ctx")
    mine = 2 * own_rows
    blocks = bias_ref.shape[0] // mine
    lanes = lax.broadcasted_iota(jnp.int32, live_ref.shape, 1)
    lane_place = lanes
    for k in range(blocks):
        device = me ^ (k // (blocks // 2)) ^ (k % (blocks // 2) * 4)
        first, second = device * own_rows, (device ^ 2) * own_rows - own_rows
        row = lax.broadcasted_iota(jnp.int32, (mine, HEAD_DIM), 0)
        place = jnp.where(row < own_rows, first, second) + row
        live = (place >= text_slots) | (place < count_ref[0])
        bias_ref[k * mine : (k + 1) * mine] = jnp.where(live, 0.0, MASKED).astype(jnp.bfloat16)
        if k == 0:
            live_own_ref[...] = live[:, :1].astype(jnp.float32)
        lane_place = jnp.where(lanes >= k * mine, first + lanes - k * mine, lane_place)
        lane_place = jnp.where(lanes >= k * mine + own_rows, second + lanes - k * mine, lane_place)
    live_ref[...] = ((lane_place >= text_slots) | (lane_place < count_ref[0])).astype(jnp.float32)


def dot_nt(a, b):
    return lax.dot_general(a, b, (((1,), (1,)), ((), ())), preferred_element_type=jnp.float32)


def fold(block, op):
    parts = [block[i : i + 8] for i in range(0, block.shape[0], 8)]
    while len(parts) > 1:
        parts = [op(*parts[i : i + 2]) if i + 1 < len(parts) else parts[i] for i in range(0, len(parts), 2)]
    return parts[0]


def part(refs, which, start, size):
    half = refs[0].shape[0]
    columns = slice(which * HEAD_DIM, (which + 1) * HEAD_DIM)
    if start + size <= half:
        return refs[0][start : start + size, columns]
    if start >= half:
        return refs[1][start - half : start - half + size, columns]
    return jnp.concatenate([refs[0][start:, columns], refs[1][: start + size - half, columns]], axis=0)


def queries(refs, which, start, size):
    one = (lax.broadcasted_iota(jnp.int32, (size, HEAD_DIM), 1) == 0).astype(jnp.bfloat16)
    return jnp.concatenate([part(refs, which, start, size), one], axis=1)


def keys(refs, bias_ref, which, start, size):
    return jnp.concatenate([part(refs, which, start, size), bias_ref[start : start + size]], axis=1)


def row_sums(items, refs, bias_ref, scores_ref, powers_ref, strip):
    half = refs[0].shape[0]

    def score(n):
        start, size, low, high = items[n]
        tops = []
        for m, which in enumerate((0, 2)):
            wide = queries(refs, which, start, size)
            top = None
            for k in range(low, high, half):
                block = dot_nt(keys(refs, bias_ref, which + 1, k, half), wide)
                scores_ref[n % 2, m, k : k + half, :size] = block
                highest = fold(block, jnp.maximum)
                top = highest if top is None else jnp.maximum(top, highest)
            tops.append(jnp.max(top, axis=0, keepdims=True))
        return tops

    tops = score(0)
    for n, (start, size, low, high) in enumerate(items):
        later = score(n + 1) if n + 1 < len(items) else None
        sums = [None] * 4
        for k in range(low, high, strip):
            source, edit = (
                jnp.exp2((scores_ref[n % 2, m, k : k + strip, :size] - tops[m]) * SHARP) for m in range(2)
            )
            if k == 0:
                powers_ref[0, :, start : start + size] = source
                powers_ref[1, :, start : start + size] = edit
            terms = [fold(t, jnp.add) for t in (source, edit, edit * edit, source * edit)]
            sums = [t if s is None else s + t for s, t in zip(sums, terms)]
        yield tops, [jnp.sum(s, axis=0, keepdims=True) for s in sums]
        tops = later


def row_chunks(start, end):
    return [(at, min(ROW_CHUNK, end - at)) for at in range(start, end, ROW_CHUNK)]


def early_kernel(own_rows, a_ref, bias_ref, stats_out, powers_out, scores_ref):
    half = a_ref.shape[0]
    items = [(start, size, 0, half) for start, size in row_chunks(0, stats_out.shape[1])]
    for (start, size, *_), (tops, sums) in zip(
        items, row_sums(items, (a_ref,), bias_ref, scores_ref, powers_out, 2 * own_rows)
    ):
        for row, value in enumerate(tops + sums):
            stats_out[row : row + 1, start : start + size] = value


def head_kernel(
    weight, own_rows, a_ref, b_ref, bias_ref, live_ref, live_own_ref, stats_ref, early_ref, keep_out, send_out,
    scores_ref, powers_ref,
):
    half = a_ref.shape[0]
    rows = 2 * half
    mine = 2 * own_rows
    scale = 1.0 / math.sqrt(HEAD_DIM)
    refs = (a_ref, b_ref)

    def own_powers(which):
        scores = dot_nt(queries(refs, which, 0, mine), keys(refs, bias_ref, which + 1, 0, rows))
        highest = jnp.max(scores, axis=1, keepdims=True)
        powers = jnp.exp2((scores - highest) * SHARP)
        return powers * (1.0 / jnp.sum(powers, axis=1, keepdims=True))

    probs_source, probs_edit = own_powers(0), own_powers(2)
    map_grad = (probs_edit - probs_source) * (2.0 * weight * live_own_ref[...])
    row_delta = jnp.sum(map_grad * probs_edit, axis=1, keepdims=True)
    grad = (probs_edit * (map_grad - row_delta)).astype(jnp.bfloat16)
    query_grad = jnp.dot(grad, part(refs, 3, 0, rows), preferred_element_type=jnp.float32) * scale

    ready = stats_ref.shape[1]
    items = [(start, size, half, rows) for start, size in row_chunks(0, ready)]
    items += [(start, size, 0, rows) for start, size in row_chunks(ready, rows)]
    total = jnp.zeros((mine, HEAD_DIM), jnp.float32)
    for (start, size, low, _), (tops, sums) in zip(
        items, row_sums(items, refs, bias_ref, scores_ref, powers_ref, mine)
    ):
        lanes = slice(start, start + size)
        if low:
            before = [stats_ref[row : row + 1, lanes] for row in range(6)]
            highest = [jnp.maximum(x, y) for x, y in zip(before, tops)]
            old, new = (
                [jnp.exp2((x - y) * SHARP) for x, y in zip(part_tops, highest)] for part_tops in (before, tops)
            )
            sums = [
                x * (old[p] * old[q] if q else old[p]) + y * (new[p] * new[q] if q else new[p])
                for x, y, p, q in zip(before[2:], sums, (0, 1, 1, 0), (0, 0, 1, 1))
            ]
            powers_source, powers_edit = early_ref[0, :, lanes] * old[0], early_ref[1, :, lanes] * old[1]
        else:
            powers_source, powers_edit = powers_ref[0, :, lanes], powers_ref[1, :, lanes]
        sum_source, sum_edit, square, cross = sums
        over_source, over_edit = 1.0 / sum_source, 1.0 / sum_edit
        factor = 2.0 * weight * live_ref[:, lanes]
        delta = factor * (square * over_edit - cross * over_source) * over_edit
        probs_edit = powers_edit * over_edit
        probs_source = powers_source * over_source
        grad = (probs_edit * (factor * (probs_edit - probs_source) - delta)).astype(jnp.bfloat16)
        total = total + jnp.dot(grad, part(refs, 2, start, size), preferred_element_type=jnp.float32)
    for columns, grad in ((slice(None, HEAD_DIM), query_grad), (slice(HEAD_DIM, None), total * scale)):
        keep_out[:, columns] = grad[:own_rows]
        send_out[:, columns] = grad[own_rows:].astype(send_out.dtype)


def local_by_heads(query_source, key_source, query_edit, key_edit, text_count):
    local_rows, full_width = query_source.shape
    size = lax.axis_size("ctx")
    all_rows = local_rows * size
    text_slots = min(TEXT_SLOTS, all_rows // 4)
    weight = 4.0 * all_rows * math.sqrt(all_rows)
    me = lax.axis_index("ctx")
    head = (me >> 1) & 1
    arrays = (query_source, key_source, query_edit, key_edit)

    def swap(array, bits):
        return lax.ppermute(array, "ctx", [(i, i ^ bits) for i in range(size)])

    pack = jax.ShapeDtypeStruct((local_rows, 4 * HEAD_DIM), jnp.bfloat16)
    own, other = pl.pallas_call(
        pack_kernel,
        out_shape=(pack, pack),
        in_specs=[HBM] * 4,
        out_specs=(VMEM, VMEM),
        scratch_shapes=[pltpu.VMEM((4, local_rows, full_width), jnp.bfloat16), pltpu.SemaphoreType.DMA((4,))],
        compiler_params=pltpu.CompilerParams(vmem_limit_bytes=4 * 1024 * 1024),
        name="pack",
    )(*(pltpu.with_memory_space_constraint(x, pltpu.HBM) for x in arrays))

    mine = 2 * local_rows
    partner = swap(other, 2)
    two = jnp.concatenate([own, partner], axis=0)
    far = [(0, own), (local_rows, partner)]
    for bit in [1 << p for p in range(size.bit_length() - 2, 2, -1)]:
        far += [(at + bit * mine // 4, swap(block, bit)) for at, block in far]
    far = far[2:]
    blocks = [(0, two), (mine, swap(two, 4))] + far + [(at + mine, swap(block, 4)) for at, block in far]
    held = jnp.concatenate([block for _, block in sorted(blocks, key=lambda entry: entry[0])], axis=0)
    held, count = lax.optimization_barrier((held, text_count))
    across = swap(held, 1)
    bias, live, live_own = pl.pallas_call(
        functools.partial(mask_kernel, local_rows, text_slots),
        out_shape=(
            jax.ShapeDtypeStruct((all_rows, HEAD_DIM), jnp.bfloat16),
            jax.ShapeDtypeStruct((1, all_rows), jnp.float32),
            jax.ShapeDtypeStruct((mine, 1), jnp.float32),
        ),
        in_specs=[SMEM],
        out_specs=(VMEM,) * 3,
        compiler_params=pltpu.CompilerParams(vmem_limit_bytes=4 * 1024 * 1024),
        name="mask",
    )(count)

    half = all_rows // 2
    ready = half // ROW_CHUNK * ROW_CHUNK
    scores = pltpu.VMEM((2, 2, all_rows, ROW_CHUNK), jnp.float32)
    stats, powers = pl.pallas_call(
        functools.partial(early_kernel, local_rows),
        out_shape=(
            jax.ShapeDtypeStruct((8, ready), jnp.float32),
            jax.ShapeDtypeStruct((2, mine, ready), jnp.float32),
        ),
        in_specs=[VMEM] * 2,
        out_specs=(VMEM, VMEM),
        scratch_shapes=[scores],
        compiler_params=pltpu.CompilerParams(vmem_limit_bytes=32 * 1024 * 1024),
        name="early",
    )(held, bias)

    grads = jax.ShapeDtypeStruct((local_rows, 2 * HEAD_DIM), jnp.float32)
    keep, send = pl.pallas_call(
        functools.partial(head_kernel, weight, local_rows),
        out_shape=(grads, grads),
        in_specs=[VMEM] * 7,
        out_specs=(VMEM, VMEM),
        scratch_shapes=[scores, pltpu.VMEM((2, mine, all_rows), jnp.float32)],
        compiler_params=pltpu.CompilerParams(vmem_limit_bytes=40 * 1024 * 1024),
        name="head",
    )(held, across, bias, live, live_own, stats, powers)
    back = swap(send, 2)

    def both_heads(columns):
        mine, other = keep[:, columns], back[:, columns]
        return jnp.where(
            head == 0, jnp.concatenate([mine, other], axis=1), jnp.concatenate([other, mine], axis=1)
        )

    return both_heads(slice(None, HEAD_DIM)), both_heads(slice(HEAD_DIM, None))


def local(query_source, key_source, query_edit, key_edit, text_count):
    local_rows, full_width = query_source.shape
    size = lax.axis_size("ctx")
    small = 2 * ROW_CHUNK <= local_rows * size <= GATHER_ALL_ROWS
    if full_width == 2 * HEAD_DIM and small and size >= 8 and size & (size - 1) == 0 and local_rows % 8 == 0:
        return local_by_heads(query_source, key_source, query_edit, key_edit, text_count)
    return local_by_rows(query_source, key_source, query_edit, key_edit, text_count)


def solution(mesh):
    split = P(("req", "ctx"), None)
    return jax.shard_map(
        local, mesh=mesh, in_specs=(split,) * 4 + (P("req"),), out_specs=(split, split), check_vma=False
    )
```

```python
import functools
import math

import jax
import jax.numpy as jnp
from jax import lax
from jax.experimental import pallas as pl
from jax.experimental.pallas import tpu as pltpu
from jax.sharding import PartitionSpec as P

HEAD_DIM = 128
TEXT_SLOTS = 512
GATHER_ALL_ROWS = 2048
MASKED = -1e30
ROW_CHUNK = 256
SHARP = math.log2(math.e) / math.sqrt(HEAD_DIM)
VMEM = pl.BlockSpec(memory_space=pltpu.VMEM)
SMEM = pl.BlockSpec(memory_space=pltpu.SMEM)
HBM = pl.BlockSpec(memory_space=pltpu.HBM)


def masked_softmax(scores, key_valid):
    masked = jnp.where(key_valid, scores, -jnp.inf)
    highest = jnp.max(masked, axis=-1, keepdims=True)
    powers = jnp.where(key_valid, jnp.exp(scores - highest), 0.0)
    totals = jnp.sum(powers, axis=-1, keepdims=True)
    return powers / totals


def local_by_rows(query_source, key_source, query_edit, key_edit, text_count):
    local_rows, full_width = query_source.shape
    head_count = full_width // HEAD_DIM
    all_rows = local_rows * lax.axis_size("ctx")
    text_slots = min(TEXT_SLOTS, all_rows // 4)
    score_scale = 1.0 / math.sqrt(HEAD_DIM)
    weight = 4.0 * all_rows * math.sqrt(all_rows)
    places = jnp.arange(all_rows)
    token_valid = (places >= text_slots) | (places < text_count[0])
    own_places = lax.axis_index("ctx") * local_rows + jnp.arange(local_rows)
    own_valid = (own_places >= text_slots) | (own_places < text_count[0])
    own_weight = own_valid.astype(jnp.float32)

    def heads_view(matrix):
        return matrix.reshape(matrix.shape[0], head_count, HEAD_DIM)

    every_ks = lax.all_gather(key_source, "ctx", axis=0, tiled=True)
    every_ke = lax.all_gather(key_edit, "ctx", axis=0, tiled=True)
    own_qs, own_qe = heads_view(query_source), heads_view(query_edit)
    dot = functools.partial(jnp.einsum, preferred_element_type=jnp.float32)
    scores_source = dot("rhd,lhd->hrl", own_qs, heads_view(every_ks)) * score_scale
    scores_edit = dot("rhd,lhd->hrl", own_qe, heads_view(every_ke)) * score_scale
    probs_source = masked_softmax(scores_source, token_valid[None, None, :])
    probs_edit = masked_softmax(scores_edit, token_valid[None, None, :])
    map_grad = 2.0 * weight * (probs_edit - probs_source) * own_weight[None, :, None]
    row_delta = jnp.sum(map_grad * probs_edit, axis=-1, keepdims=True)
    score_grad = (probs_edit * (map_grad - row_delta)).astype(jnp.bfloat16)
    query_grad = dot("hrl,lhd->rhd", score_grad, heads_view(every_ke)) * score_scale
    term_block = dot("hrl,rhd->lhd", score_grad, own_qe) * score_scale
    key_grad = lax.psum_scatter(
        term_block.reshape(all_rows, full_width), "ctx", scatter_dimension=0, tiled=True
    )
    return (query_grad.reshape(local_rows, full_width), key_grad)


def pack_kernel(qs_ref, ks_ref, qe_ref, ke_ref, own_ref, other_ref, held_ref, sems):
    copies = [
        pltpu.make_async_copy(ref, held_ref.at[place], sems.at[place])
        for place, ref in enumerate((qs_ref, ks_ref, qe_ref, ke_ref))
    ]
    for copy in copies:
        copy.start()
    first = (lax.axis_index("ctx") >> 1) & 1 == 0
    for place, copy in enumerate(copies):
        copy.wait()
        low, high = held_ref[place, :, :HEAD_DIM], held_ref[place, :, HEAD_DIM:]
        columns = slice(place * HEAD_DIM, (place + 1) * HEAD_DIM)
        own_ref[:, columns] = jnp.where(first, low, high)
        other_ref[:, columns] = jnp.where(first, high, low)


def mask_kernel(own_rows, text_slots, count_ref, bias_ref, live_ref, live_own_ref):
    me = lax.axis_index("ctx")
    mine = 2 * own_rows
    blocks = bias_ref.shape[0] // mine
    lanes = lax.broadcasted_iota(jnp.int32, live_ref.shape, 1)
    lane_place = lanes
    for k in range(blocks):
        device = me ^ (k // (blocks // 2)) ^ (k % (blocks // 2) * 4)
        first, second = device * own_rows, (device ^ 2) * own_rows - own_rows
        row = lax.broadcasted_iota(jnp.int32, (mine, HEAD_DIM), 0)
        place = jnp.where(row < own_rows, first, second) + row
        live = (place >= text_slots) | (place < count_ref[0])
        bias_ref[k * mine : (k + 1) * mine] = jnp.where(live, 0.0, MASKED).astype(jnp.bfloat16)
        if k == 0:
            live_own_ref[...] = live[:, :1].astype(jnp.float32)
        lane_place = jnp.where(lanes >= k * mine, first + lanes - k * mine, lane_place)
        lane_place = jnp.where(lanes >= k * mine + own_rows, second + lanes - k * mine, lane_place)
    live_ref[...] = ((lane_place >= text_slots) | (lane_place < count_ref[0])).astype(jnp.float32)


def dot_nt(a, b):
    return lax.dot_general(a, b, (((1,), (1,)), ((), ())), preferred_element_type=jnp.float32)


def fold(block, op):
    parts = [block[i : i + 8] for i in range(0, block.shape[0], 8)]
    while len(parts) > 1:
        parts = [op(*parts[i : i + 2]) if i + 1 < len(parts) else parts[i] for i in range(0, len(parts), 2)]
    return parts[0]


def part(refs, which, start, size):
    half = refs[0].shape[0]
    columns = slice(which * HEAD_DIM, (which + 1) * HEAD_DIM)
    if start + size <= half:
        return refs[0][start : start + size, columns]
    if start >= half:
        return refs[1][start - half : start - half + size, columns]
    return jnp.concatenate([refs[0][start:, columns], refs[1][: start + size - half, columns]], axis=0)


def queries(refs, which, start, size):
    one = (lax.broadcasted_iota(jnp.int32, (size, HEAD_DIM), 1) == 0).astype(jnp.bfloat16)
    return jnp.concatenate([part(refs, which, start, size), one], axis=1)


def keys(refs, bias_ref, which, start, size):
    return jnp.concatenate([part(refs, which, start, size), bias_ref[start : start + size]], axis=1)


def row_sums(items, refs, bias_ref, scores_ref, powers_ref, strip):
    half = refs[0].shape[0]

    def score(n):
        start, size, low, high = items[n]
        tops = []
        for m, which in enumerate((0, 2)):
            wide = queries(refs, which, start, size)
            top = None
            for k in range(low, high, half):
                block = dot_nt(keys(refs, bias_ref, which + 1, k, half), wide)
                scores_ref[n % 2, m, k : k + half, :size] = block
                highest = fold(block, jnp.maximum)
                top = highest if top is None else jnp.maximum(top, highest)
            tops.append(jnp.max(top, axis=0, keepdims=True))
        return tops

    tops = score(0)
    for n, (start, size, low, high) in enumerate(items):
        later = score(n + 1) if n + 1 < len(items) else None
        sums = [None] * 4
        for k in range(low, high, strip):
            source, edit = (
                jnp.exp2((scores_ref[n % 2, m, k : k + strip, :size] - tops[m]) * SHARP) for m in range(2)
            )
            if k == 0:
                powers_ref[0, :, start : start + size] = source
                powers_ref[1, :, start : start + size] = edit
            terms = [fold(t, jnp.add) for t in (source, edit, edit * edit, source * edit)]
            sums = [t if s is None else s + t for s, t in zip(sums, terms)]
        yield tops, [jnp.sum(s, axis=0, keepdims=True) for s in sums]
        tops = later


def row_chunks(start, end):
    return [(at, min(ROW_CHUNK, end - at)) for at in range(start, end, ROW_CHUNK)]


def early_kernel(own_rows, a_ref, bias_ref, stats_out, powers_out, scores_ref):
    half = a_ref.shape[0]
    items = [(start, size, 0, half) for start, size in row_chunks(0, stats_out.shape[1])]
    for (start, size, *_), (tops, sums) in zip(
        items, row_sums(items, (a_ref,), bias_ref, scores_ref, powers_out, 2 * own_rows)
    ):
        for row, value in enumerate(tops + sums):
            stats_out[row : row + 1, start : start + size] = value


def head_kernel(
    weight, own_rows, a_ref, b_ref, bias_ref, live_ref, live_own_ref, stats_ref, early_ref, keep_out, send_out,
    scores_ref, powers_ref,
):
    half = a_ref.shape[0]
    rows = 2 * half
    mine = 2 * own_rows
    scale = 1.0 / math.sqrt(HEAD_DIM)
    refs = (a_ref, b_ref)

    def own_powers(which):
        scores = dot_nt(queries(refs, which, 0, mine), keys(refs, bias_ref, which + 1, 0, rows))
        highest = jnp.max(scores, axis=1, keepdims=True)
        powers = jnp.exp2((scores - highest) * SHARP)
        return powers * (1.0 / jnp.sum(powers, axis=1, keepdims=True))

    probs_source, probs_edit = own_powers(0), own_powers(2)
    map_grad = (probs_edit - probs_source) * (2.0 * weight * live_own_ref[...])
    row_delta = jnp.sum(map_grad * probs_edit, axis=1, keepdims=True)
    grad = (probs_edit * (map_grad - row_delta)).astype(jnp.bfloat16)
    query_grad = jnp.dot(grad, part(refs, 3, 0, rows), preferred_element_type=jnp.float32) * scale

    ready = stats_ref.shape[1]
    items = [(start, size, half, rows) for start, size in row_chunks(0, ready)]
    items += [(start, size, 0, rows) for start, size in row_chunks(ready, rows)]
    total = jnp.zeros((mine, HEAD_DIM), jnp.float32)
    for (start, size, low, _), (tops, sums) in zip(
        items, row_sums(items, refs, bias_ref, scores_ref, powers_ref, mine)
    ):
        lanes = slice(start, start + size)
        if low:
            before = [stats_ref[row : row + 1, lanes] for row in range(6)]
            highest = [jnp.maximum(x, y) for x, y in zip(before, tops)]
            old, new = (
                [jnp.exp2((x - y) * SHARP) for x, y in zip(part_tops, highest)] for part_tops in (before, tops)
            )
            sums = [
                x * (old[p] * old[q] if q else old[p]) + y * (new[p] * new[q] if q else new[p])
                for x, y, p, q in zip(before[2:], sums, (0, 1, 1, 0), (0, 0, 1, 1))
            ]
            powers_source, powers_edit = early_ref[0, :, lanes] * old[0], early_ref[1, :, lanes] * old[1]
        else:
            powers_source, powers_edit = powers_ref[0, :, lanes], powers_ref[1, :, lanes]
        sum_source, sum_edit, square, cross = sums
        over_source, over_edit = 1.0 / sum_source, 1.0 / sum_edit
        factor = 2.0 * weight * live_ref[:, lanes]
        delta = factor * (square * over_edit - cross * over_source) * over_edit
        probs_edit = powers_edit * over_edit
        probs_source = powers_source * over_source
        grad = (probs_edit * (factor * (probs_edit - probs_source) - delta)).astype(jnp.bfloat16)
        total = total + jnp.dot(grad, part(refs, 2, start, size), preferred_element_type=jnp.float32)
    for columns, grad in ((slice(None, HEAD_DIM), query_grad), (slice(HEAD_DIM, None), total * scale)):
        keep_out[:, columns] = grad[:own_rows]
        send_out[:, columns] = grad[own_rows:].astype(send_out.dtype)


def local_by_heads(query_source, key_source, query_edit, key_edit, text_count):
    local_rows, full_width = query_source.shape
    size = lax.axis_size("ctx")
    all_rows = local_rows * size
    text_slots = min(TEXT_SLOTS, all_rows // 4)
    weight = 4.0 * all_rows * math.sqrt(all_rows)
    me = lax.axis_index("ctx")
    head = (me >> 1) & 1
    arrays = (query_source, key_source, query_edit, key_edit)

    def swap(array, bits):
        return lax.ppermute(array, "ctx", [(i, i ^ bits) for i in range(size)])

    pack = jax.ShapeDtypeStruct((local_rows, 4 * HEAD_DIM), jnp.bfloat16)
    own, other = pl.pallas_call(
        pack_kernel,
        out_shape=(pack, pack),
        in_specs=[HBM] * 4,
        out_specs=(VMEM, VMEM),
        scratch_shapes=[pltpu.VMEM((4, local_rows, full_width), jnp.bfloat16), pltpu.SemaphoreType.DMA((4,))],
        compiler_params=pltpu.CompilerParams(vmem_limit_bytes=4 * 1024 * 1024),
        name="pack",
    )(*(pltpu.with_memory_space_constraint(x, pltpu.HBM) for x in arrays))

    mine = 2 * local_rows
    partner = swap(other, 2)
    two = jnp.concatenate([own, partner], axis=0)
    far = [(0, own), (local_rows, partner)]
    for bit in [1 << p for p in range(size.bit_length() - 2, 2, -1)]:
        far += [(at + bit * mine // 4, swap(block, bit)) for at, block in far]
    far = far[2:]
    blocks = [(0, two), (mine, swap(two, 4))] + far + [(at + mine, swap(block, 4)) for at, block in far]
    held = jnp.concatenate([block for _, block in sorted(blocks, key=lambda entry: entry[0])], axis=0)
    held, count = lax.optimization_barrier((held, text_count))
    across = swap(held, 1)
    bias, live, live_own = pl.pallas_call(
        functools.partial(mask_kernel, local_rows, text_slots),
        out_shape=(
            jax.ShapeDtypeStruct((all_rows, HEAD_DIM), jnp.bfloat16),
            jax.ShapeDtypeStruct((1, all_rows), jnp.float32),
            jax.ShapeDtypeStruct((mine, 1), jnp.float32),
        ),
        in_specs=[SMEM],
        out_specs=(VMEM,) * 3,
        compiler_params=pltpu.CompilerParams(vmem_limit_bytes=4 * 1024 * 1024),
        name="mask",
    )(count)

    half = all_rows // 2
    ready = half // ROW_CHUNK * ROW_CHUNK
    scores = pltpu.VMEM((2, 2, all_rows, ROW_CHUNK), jnp.float32)
    stats, powers = pl.pallas_call(
        functools.partial(early_kernel, local_rows),
        out_shape=(
            jax.ShapeDtypeStruct((8, ready), jnp.float32),
            jax.ShapeDtypeStruct((2, mine, ready), jnp.float32),
        ),
        in_specs=[VMEM] * 2,
        out_specs=(VMEM, VMEM),
        scratch_shapes=[scores],
        compiler_params=pltpu.CompilerParams(vmem_limit_bytes=32 * 1024 * 1024),
        name="early",
    )(held, bias)

    grads = jax.ShapeDtypeStruct((local_rows, 2 * HEAD_DIM), jnp.float32)
    keep, send = pl.pallas_call(
        functools.partial(head_kernel, weight, local_rows),
        out_shape=(grads, jax.ShapeDtypeStruct(grads.shape, jnp.bfloat16)),
        in_specs=[VMEM] * 7,
        out_specs=(VMEM, VMEM),
        scratch_shapes=[scores, pltpu.VMEM((2, mine, all_rows), jnp.float32)],
        compiler_params=pltpu.CompilerParams(vmem_limit_bytes=40 * 1024 * 1024),
        name="head",
    )(held, across, bias, live, live_own, stats, powers)
    back = swap(send, 2)

    def both_heads(columns):
        mine, other = keep[:, columns], back[:, columns].astype(jnp.float32)
        return jnp.where(
            head == 0, jnp.concatenate([mine, other], axis=1), jnp.concatenate([other, mine], axis=1)
        )

    return both_heads(slice(None, HEAD_DIM)), both_heads(slice(HEAD_DIM, None))


def local(query_source, key_source, query_edit, key_edit, text_count):
    local_rows, full_width = query_source.shape
    size = lax.axis_size("ctx")
    small = 2 * ROW_CHUNK <= local_rows * size <= GATHER_ALL_ROWS
    if full_width == 2 * HEAD_DIM and small and size >= 8 and size & (size - 1) == 0 and local_rows % 8 == 0:
        return local_by_heads(query_source, key_source, query_edit, key_edit, text_count)
    return local_by_rows(query_source, key_source, query_edit, key_edit, text_count)


def solution(mesh):
    split = P(("req", "ctx"), None)
    return jax.shard_map(
        local, mesh=mesh, in_specs=(split,) * 4 + (P("req"),), out_specs=(split, split), check_vma=False
    )
```
